512 devices in a mesh: span: 32 (over z, core), local: 16 (over y, x).
Axes of the slice: x: 4, y: 4, z: 16, core: 2. Of those that a mesh axis runs over, the one named last changes fastest.
Arguments:
- queries: bfloat16 [65536, 2560], P(('span', 'local')), may hold values from -8 to 8
- keys: bfloat16 [32768, 512], P(('span', 'local')), may hold values from -8 to 8
- values: bfloat16 [32768, 512], P(('span', 'local')), may hold values from -6 to 6
- far_blocks: int32 [512, 4, 4], P(('span', 'local')), may hold values from 0 to 255, as said below
- far_live_length: int32 [512, 4], P(('span', 'local')), may hold values from 3 to 4
Outputs:
- attended: bfloat16 [65536, 2560], P(('span', 'local'))
The draws below stay inside these ranges and needn't reach their ends.
Inputs may be any that keep to these rules, and one draw needn't show every extreme that they name: `far_blocks`: entry c names key block c. Every an entry of value names a block outside the span group of its query block, and the entries of one list are distinct. Among the live entries (list position below far_live_length) of the lists of one device's 1 query block, at most 2 name blocks of any one span group, and in every draw some span group is named exactly 2 times by each device's lists. `far_live_length`: list entries at positions from the count on are ignored.
All inputs are finite; a program needn't handle non-finite values.
Results may differ from the reference program's by a relative error of at most 0.0047.
Values may be sent and summed in bfloat16 or wider, within the bound.
No kernel may reach another device: no remote copies, remote signals or barrier semaphores. Data moves between devices by JAX's collectives and lax.ppermute only.
A program may use at most 64 MiB of HBM per device.

```python
import math
import jax
import jax.numpy as jnp
from jax import lax

QUERY_HEADS = 20
KEY_HEADS = 4
HEAD_WIDTH = 128
BLOCK_WIDTH = 128
QDEV = 128
KDEV = 64
QUERY_BLOCKS_ONE = 1
FAR_ENTRIES = 4
CAP = 2
QTOK = 65536
PREFIX_TOKENS = 32768
QUERY_BLOCKS = 512
KEY_BLOCKS = 256
N_SPAN = 32
N_LOCAL = 16


def draw_queries(key, part):
    key = jax.random.fold_in(key, 1)
    start_offset = jnp.clip(jax.random.normal(key, (QTOK, QUERY_HEADS * HEAD_WIDTH), jnp.float32), -8.0, 8.0)
    return start_offset.astype(jnp.bfloat16)


def draw_keys(key, part):
    key = jax.random.fold_in(key, 2)
    start_offset = jnp.clip(jax.random.normal(key, (PREFIX_TOKENS, KEY_HEADS * HEAD_WIDTH), jnp.float32), -8.0, 8.0)
    return start_offset.astype(jnp.bfloat16)


def draw_far_blocks(key, part):
    key = jax.random.fold_in(key, 7)
    device_number = N_SPAN * N_LOCAL
    span_block_tiles = N_LOCAL * KDEV // BLOCK_WIDTH
    request_number = QUERY_BLOCKS_ONE * KEY_HEADS * FAR_ENTRIES

    def one_device(number):
        sub = jax.random.fold_in(key, number)
        home_device = number // N_LOCAL
        star = jax.random.randint(jax.random.fold_in(sub, 1), (), 0, N_SPAN - 1)
        order = jax.random.permutation(jax.random.fold_in(sub, 2), N_SPAN - 2)
        picks = jax.random.randint(jax.random.fold_in(sub, 3), (request_number,), 0, span_block_tiles)
        position = jnp.arange(request_number)
        lists = position // FAR_ENTRIES
        special = jnp.logical_and(position % FAR_ENTRIES == 0, lists < CAP)
        rank = position - jnp.minimum(CAP, lists + 1)
        pooled = order[jnp.mod(rank, N_SPAN - 2)]
        offset = jnp.where(special, star, pooled + (pooled >= star).astype(jnp.int32))
        target = (home_device + 1 + offset) % N_SPAN
        return target * span_block_tiles + picks
    row_indices = jax.vmap(one_device)(jnp.arange(device_number))
    return row_indices.reshape(device_number * QUERY_BLOCKS_ONE, KEY_HEADS, FAR_ENTRIES).astype(jnp.int32)


def touch_ends(values, stream_key, least, top_value):
    extent = values.shape
    place = [jax.random.randint(jax.random.fold_in(stream_key, axis), (), 0, extent[axis]) for axis in range(len(extent))]
    values = values.at[tuple(place)].set(least)
    longest = extent.index(max(extent))
    place[longest] = (place[longest] + 1) % extent[longest]
    return values.at[tuple(place)].set(top_value)


def shard_levels(own_key, extent, split, least, largest):
    level = 1.0
    for axis_at, shards_of in split:
        draws = jax.random.uniform(jax.random.fold_in(jax.random.fold_in(own_key, 6), axis_at), (shards_of,), jnp.float32, least / len(split), largest / len(split))
        level = level * jnp.repeat(jnp.exp(draws), extent[axis_at] // shards_of).reshape((-1,) + (1,) * (len(extent) - 1 - axis_at))
    return level


def gaussian(key, shape, scale, reach, cuts=(), held_as=jnp.bfloat16):
    drawn = scale * jax.random.normal(key, shape, jnp.float32)
    if cuts:
        drawn = drawn * shard_levels(key, shape, cuts, -0.22, 0.18)
    return jnp.clip(drawn, -reach, reach).astype(held_as)


def setup_inputs(seed: int = 0) -> dict:
    streams_of = jax.random.split(jax.random.key(seed), 6)
    queries = draw_queries(jax.random.fold_in(streams_of[5], 71), 0)
    keys = draw_keys(jax.random.fold_in(streams_of[5], 71), 0)
    values = gaussian(streams_of[2], (PREFIX_TOKENS, KEY_HEADS * HEAD_WIDTH), 1.0, 6.0, ((0, 512),))
    far_blocks = draw_far_blocks(jax.random.fold_in(streams_of[5], 71), 0)
    far_live_length = touch_ends(jax.random.randint(streams_of[4], (QUERY_BLOCKS, KEY_HEADS), FAR_ENTRIES - 1, FAR_ENTRIES + 1), jax.random.fold_in(streams_of[4], 1), FAR_ENTRIES - 1, FAR_ENTRIES).astype(jnp.int32)
    return dict(queries=queries, keys=keys, values=values, far_blocks=far_blocks, far_live_length=far_live_length)


def reference(queries, keys, values, far_blocks, far_live_length):
    head_group = QUERY_HEADS // KEY_HEADS
    span_key_rows = N_LOCAL * KDEV
    span_block_tiles = span_key_rows // BLOCK_WIDTH
    per_span = QDEV // BLOCK_WIDTH * N_LOCAL
    scale = 1.0 / math.sqrt(HEAD_WIDTH)
    key_block_tiles = keys.reshape(KEY_BLOCKS, BLOCK_WIDTH, KEY_HEADS, HEAD_WIDTH).transpose(2, 0, 1, 3)
    value_block_tiles = values.reshape(KEY_BLOCKS, BLOCK_WIDTH, KEY_HEADS, HEAD_WIDTH).transpose(2, 0, 1, 3)
    query_block_tiles = queries.reshape(QUERY_BLOCKS, BLOCK_WIDTH, KEY_HEADS, head_group, HEAD_WIDTH)
    head_number = jnp.arange(KEY_HEADS, dtype=jnp.int32)[:, None]

    def one_block(inputs):
        query_tile, blocks, counts, number = inputs
        home_device = (number // per_span).astype(jnp.int32)
        near_key_rows = lax.dynamic_slice_in_dim(key_block_tiles, home_device * span_block_tiles, span_block_tiles, 1).reshape(KEY_HEADS, span_key_rows, HEAD_WIDTH)
        near_value_rows = lax.dynamic_slice_in_dim(value_block_tiles, home_device * span_block_tiles, span_block_tiles, 1).reshape(KEY_HEADS, span_key_rows, HEAD_WIDTH)
        far_key_rows = key_block_tiles[head_number, blocks]
        far_value_rows = value_block_tiles[head_number, blocks]
        query_f = query_tile.astype(jnp.float32)
        near_s = jnp.einsum('qhgd,hkd->hgqk', query_f, near_key_rows.astype(jnp.float32)) * scale
        far_s = jnp.einsum('qhgd,hfkd->hgqfk', query_f, far_key_rows.astype(jnp.float32)) * scale
        live_entries = jnp.arange(FAR_ENTRIES, dtype=jnp.int32)[None, :] < counts[:, None]
        mask = live_entries[:, None, None, :, None]
        far_s = jnp.where(mask, far_s, -1e+30)
        top = jnp.maximum(lax.optimization_barrier(jnp.max(near_s, axis=-1)), lax.optimization_barrier(jnp.max(far_s, axis=(-2, -1))))
        near_w = jnp.exp(near_s - top[..., None])
        far_w = jnp.where(mask, jnp.exp(far_s - top[..., None, None]), 0.0)
        total = lax.optimization_barrier(jnp.sum(near_w, axis=-1)) + lax.optimization_barrier(jnp.sum(far_w, axis=(-2, -1)))
        near_b = near_w.astype(jnp.bfloat16).astype(jnp.float32)
        far_b = far_w.astype(jnp.bfloat16).astype(jnp.float32)
        acc = jnp.einsum('hgqk,hkd->hgqd', near_b, near_value_rows.astype(jnp.float32))
        acc = acc + jnp.einsum('hgqfk,hfkd->hgqd', far_b, far_value_rows.astype(jnp.float32))
        result = acc / total[..., None]
        return result.transpose(2, 0, 1, 3).reshape(BLOCK_WIDTH, QUERY_HEADS * HEAD_WIDTH).astype(jnp.bfloat16)
    numbers = jnp.arange(QUERY_BLOCKS, dtype=jnp.int32)
    outputs = lax.map(one_block, (query_block_tiles, far_blocks, far_live_length, numbers))
    return outputs.reshape(QTOK, QUERY_HEADS * HEAD_WIDTH)
```

```python
import functools
import math

import jax
import jax.numpy as jnp
from jax import lax
from jax.experimental import pallas as pl
from jax.experimental.pallas import tpu as pltpu
from jax.sharding import Mesh, PartitionSpec as P

KEY_HEADS = 4
GROUP = 5
WIDTH = 128
BLOCK = 128
LIST = 4
Z, C, Y, X = 16, 2, 4, 4
LAYER = C * Y * X
KDEV = 64
ROWS = KDEV // LAYER
SHARE = 4
NEAR = Y * X * KDEV
LANES = KEY_HEADS * 2 * WIDTH
UNIT = LAYER * ROWS
SCALE = 1.0 / math.sqrt(WIDTH)
QROWS = GROUP * BLOCK


def stack_heads(q_ref):
    return jnp.concatenate([q_ref[:, h * WIDTH : (h + 1) * WIDTH] for h in range(GROUP)], axis=0)


def near_kernel(q_ref, k_ref, v_ref, acc_ref, stat_ref):
    q = stack_heads(q_ref)
    s = lax.dot_general(
        q, k_ref[...], (((1,), (1,)), ((), ())), preferred_element_type=jnp.float32
    ) * SCALE
    top = jnp.max(s, axis=1, keepdims=True)
    w = jnp.exp(s - top)
    total = jnp.sum(w, axis=1, keepdims=True)
    acc_ref[0] = jnp.dot(w.astype(jnp.bfloat16), v_ref[...], preferred_element_type=jnp.float32)
    lane = lax.broadcasted_iota(jnp.int32, (QROWS, WIDTH), 1)
    stat_ref[0] = jnp.where(lane == 0, top, total)


def near_attention(queries, near):
    return pl.pallas_call(
        near_kernel,
        grid=(KEY_HEADS,),
        in_specs=[
            pl.BlockSpec((BLOCK, GROUP * WIDTH), lambda e: (0, e)),
            pl.BlockSpec((NEAR, WIDTH), lambda e: (0, 2 * e)),
            pl.BlockSpec((NEAR, WIDTH), lambda e: (0, 2 * e + 1)),
        ],
        out_specs=[
            pl.BlockSpec((1, QROWS, WIDTH), lambda e: (e, 0, 0)),
            pl.BlockSpec((1, QROWS, WIDTH), lambda e: (e, 0, 0)),
        ],
        out_shape=[
            jax.ShapeDtypeStruct((KEY_HEADS, QROWS, WIDTH), jnp.float32),
            jax.ShapeDtypeStruct((KEY_HEADS, QROWS, WIDTH), jnp.float32),
        ],
        compiler_params=pltpu.CompilerParams(vmem_limit_bytes=40 * 1024 * 1024),
        cost_estimate=pl.CostEstimate(
            flops=4 * KEY_HEADS * QROWS * NEAR * WIDTH,
            bytes_accessed=8 * 1024 * 1024,
            transcendentals=KEY_HEADS * QROWS * NEAR,
        ),
        name="near",
    )(queries, near, near)


def far_kernel(live_ref, q_ref, k_ref, v_ref, acc_ref, stat_ref, out_ref):
    q = stack_heads(q_ref)
    s = lax.dot_general(
        q, k_ref[...], (((1,), (1,)), ((), ())), preferred_element_type=jnp.float32
    ) * SCALE
    column = lax.broadcasted_iota(jnp.int32, (1, LIST * BLOCK), 1)
    entry = (column % (LIST * SHARE)) // SHARE
    s = jnp.where(entry < live_ref[pl.program_id(0)], s, -1e30)
    near_top = stat_ref[0][:, 0:1]
    near_total = stat_ref[0][:, 1:2]
    top = jnp.maximum(near_top, jnp.max(s, axis=1, keepdims=True))
    w = jnp.exp(s - top)
    back = jnp.exp(near_top - top)
    total = back * near_total + jnp.sum(w, axis=1, keepdims=True)
    acc = back * acc_ref[0] + jnp.dot(
        w.astype(jnp.bfloat16), v_ref[...], preferred_element_type=jnp.float32
    )
    res = (acc / total).astype(jnp.bfloat16)
    for h in range(GROUP):
        out_ref[:, h * WIDTH : (h + 1) * WIDTH] = res[h * BLOCK : (h + 1) * BLOCK]


def far_attention(live, queries, far, acc, stat):
    return pl.pallas_call(
        far_kernel,
        grid_spec=pltpu.PrefetchScalarGridSpec(
            num_scalar_prefetch=1,
            grid=(KEY_HEADS,),
            in_specs=[
                pl.BlockSpec((BLOCK, GROUP * WIDTH), lambda e, live: (0, e)),
                pl.BlockSpec((LIST * BLOCK, WIDTH), lambda e, live: (0, 2 * e)),
                pl.BlockSpec((LIST * BLOCK, WIDTH), lambda e, live: (0, 2 * e + 1)),
                pl.BlockSpec((1, QROWS, WIDTH), lambda e, live: (e, 0, 0)),
                pl.BlockSpec((1, QROWS, WIDTH), lambda e, live: (e, 0, 0)),
            ],
            out_specs=pl.BlockSpec((BLOCK, GROUP * WIDTH), lambda e, live: (0, e)),
        ),
        out_shape=jax.ShapeDtypeStruct((BLOCK, KEY_HEADS * GROUP * WIDTH), jnp.bfloat16),
        compiler_params=pltpu.CompilerParams(vmem_limit_bytes=40 * 1024 * 1024),
        name="far",
    )(live, queries, far, far, acc, stat)


def pick_kernel(index_ref, *refs):
    units, out_ref = refs[:-1], refs[-1]
    picked_rows = LAYER * LIST * SHARE
    lane = lax.broadcasted_iota(jnp.int32, (picked_rows, UNIT * Z), 1)
    for e in range(KEY_HEADS):
        hot = jnp.where(lane == index_ref[:, e : e + 1], 1.0, 0.0).astype(jnp.bfloat16)
        lanes = slice(2 * WIDTH * e, 2 * WIDTH * (e + 1))
        table = jnp.concatenate([u[:, lanes] for u in units], axis=0)
        out_ref[:, lanes] = jnp.dot(hot, table, preferred_element_type=jnp.float32).astype(
            jnp.bfloat16
        )


def pick(index, units):
    return pl.pallas_call(
        pick_kernel,
        out_shape=jax.ShapeDtypeStruct((LAYER * LIST * SHARE, LANES), jnp.bfloat16),
        compiler_params=pltpu.CompilerParams(vmem_limit_bytes=40 * 1024 * 1024),
        name="pick",
    )(index, *units)


def local(queries, keys, values, far_blocks, far_live_length):
    z = lax.axis_index("z")
    both = jnp.stack(
        [keys.reshape(KDEV, KEY_HEADS, WIDTH), values.reshape(KDEV, KEY_HEADS, WIDTH)], axis=2
    ).reshape(KDEV, LANES)
    near = lax.all_gather(both, ("y", "x"), axis=0, tiled=True)

    ids = far_blocks.reshape(1, KEY_HEADS * LIST).astype(jnp.bfloat16)
    ids = jnp.broadcast_to(jnp.pad(ids, ((0, 0), (0, WIDTH - KEY_HEADS * LIST))), (KDEV, WIDTH))
    sent = jnp.concatenate([both, ids], axis=1).reshape(LAYER, ROWS, LANES + WIDTH)
    got = lax.all_to_all(sent, ("c", "y", "x"), 0, 0, tiled=True)
    unit = got[:, :, :LANES].reshape(UNIT, LANES)
    asked = got[:, 0, LANES : LANES + KEY_HEADS * LIST].astype(jnp.int32)

    ups = [unit]
    downs = [unit]
    up = [(k, (k + 1) % Z) for k in range(Z)]
    down = [(k, (k - 1) % Z) for k in range(Z)]
    for step in range(Z // 2):
        ups.append(lax.ppermute(ups[-1], "z", up))
        if step < Z // 2 - 1:
            downs.append(lax.ppermute(downs[-1], "z", down))
    units = downs + ups[:0:-1]

    asked = asked.reshape(LAYER, KEY_HEADS, LIST, 1)
    place = (asked // (C * 8) - z) % Z
    row = (place * (C * 8) + asked % (C * 8)) * SHARE + jnp.arange(SHARE, dtype=jnp.int32)
    index = row.transpose(0, 2, 3, 1).reshape(LAYER * LIST * SHARE, KEY_HEADS)

    picked = pick(index, units)
    picked, queries = lax.optimization_barrier((picked, queries))
    arrived = lax.all_to_all(
        picked.reshape(LAYER, LIST * SHARE, LANES), ("c", "y", "x"), 0, 0, tiled=True
    )
    acc, stat = near_attention(queries, near)
    live = far_live_length.reshape(KEY_HEADS)
    return far_attention(live, queries, arrived.reshape(LIST * BLOCK, LANES), acc, stat)


def solution(mesh):
    fine = Mesh(mesh.devices.reshape(Z, C, Y, X), ("z", "c", "y", "x"))
    axes = ("z", "c", "y", "x")
    placed = (
        P(axes, None),
        P(axes, None),
        P(axes, None),
        P(axes, None, None),
        P(axes, None),
    )
    return jax.shard_map(
        local, mesh=fine, in_specs=placed, out_specs=P(axes, None), check_vma=False
    )
```

```python
import functools
import math

import jax
import jax.numpy as jnp
from jax import lax
from jax.experimental import pallas as pl
from jax.experimental.pallas import tpu as pltpu
from jax.sharding import Mesh, PartitionSpec as P

KEY_HEADS = 4
GROUP = 5
WIDTH = 128
BLOCK = 128
LIST = 4
ZH, ZL, C, Y, X = 8, 2, 2, 4, 4
PEERS = ZL * C * Y * X
PEER_AXES = ("zl", "c", "y", "x")
KDEV = 64
SHARE = 2
NEAR = Y * X * KDEV
LANES = KEY_HEADS * 2 * WIDTH
HALF = LANES // 2
UNIT = PEERS * SHARE
MAIN = UNIT - 16
REST = UNIT - MAIN
BLOCKS_PAIR = 32
PICKED = PEERS * LIST * SHARE
SCALE_LOG2 = math.log2(math.e) / math.sqrt(WIDTH)
MIB = 1024 * 1024
QROWS = GROUP * BLOCK


def stack_heads(q_ref):
    return jnp.concatenate([q_ref[:, h * WIDTH : (h + 1) * WIDTH] for h in range(GROUP)], axis=0)


def near_kernel(q_ref, k_ref, v_ref, acc_ref, stat_ref):
    q = stack_heads(q_ref)
    s = lax.dot_general(
        q, k_ref[...], (((1,), (1,)), ((), ())), preferred_element_type=jnp.float32
    )
    top = jnp.max(s, axis=1, keepdims=True)
    w = jnp.exp2((s - top) * SCALE_LOG2)
    total = jnp.sum(w, axis=1, keepdims=True)
    acc_ref[0] = jnp.dot(w.astype(jnp.bfloat16), v_ref[...], preferred_element_type=jnp.float32)
    lane = lax.broadcasted_iota(jnp.int32, (QROWS, WIDTH), 1)
    stat_ref[0] = jnp.where(lane == 0, top, total)


def near_attention(queries, near):
    return pl.pallas_call(
        near_kernel,
        grid=(KEY_HEADS,),
        in_specs=[
            pl.BlockSpec((BLOCK, GROUP * WIDTH), lambda e: (0, e)),
            pl.BlockSpec((NEAR, WIDTH), lambda e: (0, 2 * e)),
            pl.BlockSpec((NEAR, WIDTH), lambda e: (0, 2 * e + 1)),
        ],
        out_specs=[
            pl.BlockSpec((1, QROWS, WIDTH), lambda e: (e, 0, 0)),
            pl.BlockSpec((1, QROWS, WIDTH), lambda e: (e, 0, 0)),
        ],
        out_shape=[
            jax.ShapeDtypeStruct((KEY_HEADS, QROWS, WIDTH), jnp.float32),
            jax.ShapeDtypeStruct((KEY_HEADS, QROWS, WIDTH), jnp.float32),
        ],
        compiler_params=pltpu.CompilerParams(vmem_limit_bytes=16 * MIB),
        cost_estimate=pl.CostEstimate(
            flops=4 * KEY_HEADS * QROWS * NEAR * WIDTH,
            bytes_accessed=8 * 1024 * 1024,
            transcendentals=KEY_HEADS * QROWS * NEAR,
        ),
        name="near",
    )(queries, near, near)


def far_kernel(live_ref, q_ref, far_ref, acc_ref, stat_ref, out_ref):
    column = lax.broadcasted_iota(jnp.int32, (1, LIST * BLOCK), 1)
    entry = (column % (LIST * SHARE)) // SHARE
    for e in range(KEY_HEADS):
        k = far_ref[:, 2 * e * WIDTH : (2 * e + 1) * WIDTH]
        v = far_ref[:, (2 * e + 1) * WIDTH : (2 * e + 2) * WIDTH]
        mask = entry < live_ref[e]
        q = jnp.concatenate(
            [
                q_ref[:, (e * GROUP + h) * WIDTH : (e * GROUP + h + 1) * WIDTH]
                for h in range(GROUP)
            ],
            axis=0,
        )
        s = lax.dot_general(q, k, (((1,), (1,)), ((), ())), preferred_element_type=jnp.float32)
        s = jnp.where(mask, s, -1e30)
        near_top = stat_ref[e, :, 0:1]
        near_total = stat_ref[e, :, 1:2]
        top = jnp.maximum(near_top, jnp.max(s, axis=1, keepdims=True))
        w = jnp.exp2((s - top) * SCALE_LOG2)
        back = jnp.exp2((near_top - top) * SCALE_LOG2)
        total = back * near_total + jnp.sum(w, axis=1, keepdims=True)
        acc = back * acc_ref[e] + jnp.dot(
            w.astype(jnp.bfloat16), v, preferred_element_type=jnp.float32
        )
        res = (acc / total).astype(jnp.bfloat16)
        for h in range(GROUP):
            head = slice((e * GROUP + h) * WIDTH, (e * GROUP + h + 1) * WIDTH)
            out_ref[:, head] = res[h * BLOCK : (h + 1) * BLOCK]


def far_attention(live, queries, far, acc, stat):
    vmem = pl.BlockSpec(memory_space=pltpu.VMEM)
    return pl.pallas_call(
        far_kernel,
        in_specs=[pl.BlockSpec(memory_space=pltpu.SMEM), vmem, vmem, vmem, vmem],
        out_specs=vmem,
        out_shape=jax.ShapeDtypeStruct((BLOCK, KEY_HEADS * GROUP * WIDTH), jnp.bfloat16),
        compiler_params=pltpu.CompilerParams(vmem_limit_bytes=16 * MIB),
        name="far",
    )(live, queries, far, acc, stat)


def pick_kernel(index_ref, main_ref, rest_ref, out_ref):
    lane = lax.broadcasted_iota(jnp.int32, (PICKED, UNIT * ZH), 1)
    for e in range(KEY_HEADS):
        hot = jnp.where(lane == index_ref[:, e : e + 1], 1.0, 0.0).astype(jnp.bfloat16)
        source = slice(2 * WIDTH * (e % 2), 2 * WIDTH * (e % 2 + 1))
        table = jnp.concatenate([main_ref[:, source], rest_ref[:, source]], axis=0)
        out_ref[:, 2 * WIDTH * e : 2 * WIDTH * (e + 1)] = jnp.dot(
            hot, table, preferred_element_type=jnp.float32
        ).astype(jnp.bfloat16)


def pick(index, main, rest):
    return pl.pallas_call(
        pick_kernel,
        out_shape=jax.ShapeDtypeStruct((PICKED, LANES), jnp.bfloat16),
        compiler_params=pltpu.CompilerParams(vmem_limit_bytes=16 * MIB),
        name="pick",
    )(index, main, rest)


def local(queries, keys, values, far_blocks, far_live_length):
    odd = lax.axis_index("x") % 2
    both = jnp.stack(
        [keys.reshape(KDEV, KEY_HEADS, WIDTH), values.reshape(KDEV, KEY_HEADS, WIDTH)], axis=2
    ).reshape(KDEV, LANES)
    near = lax.all_gather(both, ("y", "x"), axis=0, tiled=True)

    low, high = both[:, :HALF], both[:, HALF:]
    pairs = jnp.stack([jnp.where(odd, high, low), jnp.where(odd, low, high)], axis=0)
    pairs = pairs.reshape(2, PEERS // 2, SHARE, HALF).transpose(1, 0, 2, 3)
    pairs = pairs.reshape(PEERS, SHARE, HALF)
    ids = far_blocks.reshape(1, 1, KEY_HEADS * LIST).astype(jnp.bfloat16)
    ids = jnp.pad(ids, ((0, 0), (0, 0), (0, WIDTH - KEY_HEADS * LIST)))
    ids = jnp.broadcast_to(ids, (PEERS, SHARE, WIDTH))
    got = lax.all_to_all(
        jnp.concatenate([pairs, ids], axis=2), PEER_AXES, 0, 0, tiled=True
    )
    unit = got[:, :, :HALF].reshape(UNIT, HALF)
    asked = got[:, 0, HALF : HALF + KEY_HEADS * LIST].astype(jnp.int32)

    rest = jnp.broadcast_to(unit[None, MAIN:], (ZH, REST, HALF)).reshape(ZH * REST, HALF)
    rest = lax.all_to_all(rest, "zh", 0, 0, tiled=True)
    main = lax.all_gather(unit[:MAIN], "zh", axis=0, tiled=True)

    asked = asked.reshape(PEERS, KEY_HEADS, LIST, 1)
    head_pair = jnp.arange(KEY_HEADS, dtype=jnp.int32).reshape(KEY_HEADS, 1, 1) // 2
    row = ((asked % BLOCKS_PAIR) * 2 + (head_pair ^ odd)) * SHARE
    row = row + jnp.arange(SHARE, dtype=jnp.int32)
    place = asked // BLOCKS_PAIR
    row = jnp.where(row < MAIN, place * MAIN + row, ZH * MAIN + place * REST + row - MAIN)
    index = row.transpose(0, 2, 3, 1).reshape(PICKED, KEY_HEADS)

    picked = pick(index, main, rest)
    picked, queries, near = lax.optimization_barrier((picked, queries, near))
    arrived = lax.all_to_all(
        picked.reshape(PEERS, LIST * SHARE, LANES), PEER_AXES, 0, 0, tiled=True
    )
    acc, stat = near_attention(queries, near)
    live = far_live_length.reshape(KEY_HEADS)
    return far_attention(live, queries, arrived.reshape(LIST * BLOCK, LANES), acc, stat)


def solution(mesh):
    axes = ("zh", "zl", "c", "y", "x")
    fine = Mesh(mesh.devices.reshape(ZH, ZL, C, Y, X), axes)
    placed = (
        P(axes, None),
        P(axes, None),
        P(axes, None),
        P(axes, None, None),
        P(axes, None),
    )
    return jax.shard_map(
        local, mesh=fine, in_specs=placed, out_specs=P(axes, None), check_vma=False
    )
```

```python
import functools
import math

import jax
import jax.numpy as jnp
from jax import lax
from jax.experimental import pallas as pl
from jax.experimental.pallas import tpu as pltpu
from jax.sharding import Mesh, PartitionSpec as P

KEY_HEADS = 4
GROUP = 5
WIDTH = 128
BLOCK = 128
LIST = 4
ZH, ZL, C, Y, X = 4, 4, 2, 4, 4
PEERS = ZL * C * Y * X
PEER_AXES = ("zl", "c", "y", "x")
KDEV = 64
NEAR = Y * X * KDEV
LANES = KEY_HEADS * 2 * WIDTH
PAIR = LANES // 2
TILES = PAIR // WIDTH
CHUNK = 8
SHARE = 2
PICKED = PEERS * LIST * SHARE
SCALE_LOG2 = math.log2(math.e) / math.sqrt(WIDTH)
MIB = 1024 * 1024
QROWS = GROUP * BLOCK


def stack_heads(q_ref):
    return jnp.concatenate([q_ref[:, h * WIDTH : (h + 1) * WIDTH] for h in range(GROUP)], axis=0)


def weigh(s, top):
    tiles = [
        jnp.exp2((s[:, k * WIDTH : (k + 1) * WIDTH] - top) * SCALE_LOG2)
        for k in range(s.shape[1] // WIDTH)
    ]
    return jnp.concatenate(tiles, axis=1).astype(jnp.bfloat16)


def row_top(s):
    top = s[:, :WIDTH]
    for k in range(1, s.shape[1] // WIDTH):
        top = jnp.maximum(top, s[:, k * WIDTH : (k + 1) * WIDTH])
    return jnp.broadcast_to(jnp.max(top, axis=1, keepdims=True), top.shape)


def weighted(w, v):
    ones = jnp.ones((v.shape[0], WIDTH), jnp.bfloat16)
    return jnp.dot(w, jnp.concatenate([v, ones], axis=1), preferred_element_type=jnp.float32)


def scores(q, k):
    return lax.dot_general(q, k, (((1,), (1,)), ((), ())), preferred_element_type=jnp.float32)


def diagonal():
    shape = (BLOCK, WIDTH)
    return lax.broadcasted_iota(jnp.int32, shape, 0) == lax.broadcasted_iota(jnp.int32, shape, 1)


def near_kernel(q_ref, k_ref, v_ref, mean_ref, log_ref):
    s = scores(stack_heads(q_ref), k_ref[...])
    top = row_top(s)
    both = weighted(weigh(s, top), v_ref[...])
    total = both[:, WIDTH:]
    mean_ref[0] = both[:, :WIDTH] / total
    log_ref[0] = jnp.zeros((8, WIDTH), jnp.float32)
    log = top + jnp.log2(total) * (1.0 / SCALE_LOG2)
    for h in range(GROUP):
        own = jnp.where(diagonal(), log[h * BLOCK : (h + 1) * BLOCK], 0.0)
        log_ref[0, h : h + 1] = jnp.sum(own, axis=0, keepdims=True)


def near_attention(queries, near):
    return pl.pallas_call(
        near_kernel,
        grid=(KEY_HEADS,),
        in_specs=[
            pl.BlockSpec((BLOCK, GROUP * WIDTH), lambda e: (0, e)),
            pl.BlockSpec((NEAR, WIDTH), lambda e: (0, 2 * e)),
            pl.BlockSpec((NEAR, WIDTH), lambda e: (0, 2 * e + 1)),
        ],
        out_specs=[
            pl.BlockSpec((1, QROWS, WIDTH), lambda e: (e, 0, 0)),
            pl.BlockSpec((1, 8, WIDTH), lambda e: (e, 0, 0)),
        ],
        out_shape=[
            pltpu.VMEM((KEY_HEADS, QROWS, WIDTH), jnp.float32),
            pltpu.VMEM((KEY_HEADS, 8, WIDTH), jnp.float32),
        ],
        compiler_params=pltpu.CompilerParams(vmem_limit_bytes=16 * MIB),
        cost_estimate=pl.CostEstimate(
            flops=200 * KEY_HEADS * QROWS * NEAR * WIDTH,
            bytes_accessed=8 * MIB,
            transcendentals=KEY_HEADS * QROWS * NEAR,
        ),
        name="near",
    )(
        pltpu.with_memory_space_constraint(queries, pltpu.HBM),
        pltpu.with_memory_space_constraint(near, pltpu.HBM),
        pltpu.with_memory_space_constraint(near, pltpu.HBM),
    )


def far_kernel(live_ref, q_ref, far_ref, mean_ref, log_ref, out_ref):
    column = lax.broadcasted_iota(jnp.int32, (1, LIST * BLOCK), 1)
    entry = (column % (LIST * SHARE)) // SHARE
    for e in range(KEY_HEADS):
        rows = slice(e // 2 * LIST * BLOCK, (e // 2 + 1) * LIST * BLOCK)
        k = far_ref[rows, 2 * (e % 2) * WIDTH : (2 * (e % 2) + 1) * WIDTH]
        v = far_ref[rows, (2 * (e % 2) + 1) * WIDTH : (2 * (e % 2) + 2) * WIDTH]
        q = stack_heads(q_ref.at[:, e * GROUP * WIDTH : (e + 1) * GROUP * WIDTH])
        s = jnp.where(entry < live_ref[e], scores(q, k), -1e30)
        near_log = jnp.concatenate(
            [
                jnp.broadcast_to(
                    jnp.sum(
                        jnp.where(diagonal(), log_ref[e, h : h + 1], 0.0), axis=1, keepdims=True
                    ),
                    (BLOCK, WIDTH),
                )
                for h in range(GROUP)
            ],
            axis=0,
        )
        top = jnp.maximum(near_log, row_top(s))
        back = jnp.exp2((near_log - top) * SCALE_LOG2)
        both = weighted(weigh(s, top), v)
        acc = back * mean_ref[e] + both[:, :WIDTH]
        total = back + both[:, WIDTH:]
        res = (acc / total).astype(jnp.bfloat16)
        for h in range(GROUP):
            head = slice((e * GROUP + h) * WIDTH, (e * GROUP + h + 1) * WIDTH)
            out_ref[:, head] = res[h * BLOCK : (h + 1) * BLOCK]


def far_attention(live, queries, far, mean, log):
    vmem = pl.BlockSpec(memory_space=pltpu.VMEM)
    return pl.pallas_call(
        far_kernel,
        in_specs=[pl.BlockSpec(memory_space=pltpu.SMEM), vmem, vmem, vmem, vmem],
        out_specs=vmem,
        out_shape=jax.ShapeDtypeStruct((BLOCK, KEY_HEADS * GROUP * WIDTH), jnp.bfloat16),
        compiler_params=pltpu.CompilerParams(vmem_limit_bytes=16 * MIB),
        name="far",
    )(
        live,
        queries,
        far,
        pltpu.with_memory_space_constraint(mean, pltpu.VMEM),
        pltpu.with_memory_space_constraint(log, pltpu.VMEM),
    )


def prep_kernel(ids_ref, k_ref, v_ref, near_ref, sent_ref):
    tiles = []
    for e in range(KEY_HEADS):
        tiles.append(k_ref[:, e * WIDTH : (e + 1) * WIDTH])
        tiles.append(v_ref[:, e * WIDTH : (e + 1) * WIDTH])
    near_ref[...] = jnp.concatenate(tiles, axis=1)
    shape = (KDEV * CHUNK, KDEV * TILES)
    row = lax.broadcasted_iota(jnp.int32, shape, 0)
    column = lax.broadcasted_iota(jnp.int32, shape, 1)
    target = jnp.where(row % CHUNK < TILES, row % CHUNK * KDEV + row // CHUNK, -1)
    hot = jnp.where(column == target, 1.0, 0.0).astype(jnp.bfloat16)
    shape = (KDEV * CHUNK, WIDTH)
    lane = lax.broadcasted_iota(jnp.int32, shape, 1)
    is_id = lax.broadcasted_iota(jnp.int32, shape, 0) % CHUNK >= TILES
    ids = jnp.zeros(shape, jnp.float32)
    for i in range(KEY_HEADS * LIST):
        ids = jnp.where(lane == i, ids_ref[i].astype(jnp.float32), ids)
    for j in range(2):
        moved = jnp.dot(
            hot,
            jnp.concatenate(tiles[j * TILES : (j + 1) * TILES], axis=0),
            preferred_element_type=jnp.float32,
        )
        rows = slice(j * KDEV * CHUNK, (j + 1) * KDEV * CHUNK)
        sent_ref[rows] = jnp.where(is_id, ids, moved).astype(jnp.bfloat16)


def prep(ids, keys, values):
    whole = lambda shape: pl.BlockSpec(shape, lambda i: (0, 0))
    return pl.pallas_call(
        prep_kernel,
        grid=(1,),
        in_specs=[
            pl.BlockSpec(memory_space=pltpu.SMEM),
            whole((KDEV, LANES // 2)),
            whole((KDEV, LANES // 2)),
        ],
        out_specs=[whole((KDEV, LANES)), whole((PEERS * CHUNK, WIDTH))],
        out_shape=[
            jax.ShapeDtypeStruct((KDEV, LANES), jnp.bfloat16),
            jax.ShapeDtypeStruct((PEERS * CHUNK, WIDTH), jnp.bfloat16),
        ],
        compiler_params=pltpu.CompilerParams(vmem_limit_bytes=16 * MIB),
        name="prep",
    )(
        ids,
        pltpu.with_memory_space_constraint(keys, pltpu.HBM),
        pltpu.with_memory_space_constraint(values, pltpu.HBM),
    )


def pick_kernel(index_ref, table_ref, out_ref):
    lane = lax.broadcasted_iota(jnp.int32, (PICKED, PEERS * ZH), 1)
    for e in range(2):
        hot = jnp.where(lane == index_ref[:, e : e + 1], 1.0, 0.0).astype(jnp.bfloat16)
        lanes = slice(2 * WIDTH * e, 2 * WIDTH * (e + 1))
        out_ref[:, lanes] = jnp.dot(
            hot, table_ref[:, lanes], preferred_element_type=jnp.float32
        ).astype(jnp.bfloat16)


def pick(index, table):
    return pl.pallas_call(
        pick_kernel,
        out_shape=jax.ShapeDtypeStruct((PICKED, PAIR), jnp.bfloat16),
        compiler_params=pltpu.CompilerParams(vmem_limit_bytes=16 * MIB),
        name="pick",
    )(index, table)


def local(queries, keys, values, far_blocks, far_live_length):
    near, sent = prep(far_blocks.reshape(KEY_HEADS * LIST), keys, values)
    near = lax.all_gather(near, ("y", "x"), axis=0, tiled=True)
    got = lax.all_to_all(sent.reshape(PEERS, CHUNK, WIDTH), PEER_AXES, 0, 0, tiled=True)
    table = lax.all_gather(got[:, :TILES].reshape(PEERS, PAIR), "zh", axis=0, tiled=True)

    asked = got[:, TILES, : KEY_HEADS * LIST].astype(jnp.int32).reshape(PEERS, 2, 2, LIST)
    asked = jnp.where(lax.axis_index("zl") < ZL // 2, asked[:, 0], asked[:, 1])
    half = jnp.arange(SHARE, dtype=jnp.int32).reshape(1, 1, SHARE, 1)
    index = asked.transpose(0, 2, 1)[:, :, None] * SHARE + half
    picked = pick(index.reshape(PICKED, 2), table)

    picked, queries = lax.optimization_barrier((picked, queries))
    arrived = lax.all_to_all(
        picked.reshape(PEERS, LIST * SHARE, PAIR), PEER_AXES, 0, 0, tiled=True
    )
    mean, log = near_attention(queries, near)
    live = far_live_length.reshape(KEY_HEADS)
    return far_attention(live, queries, arrived.reshape(PICKED, PAIR), mean, log)


def solution(mesh):
    axes = ("zh", "zl", "c", "y", "x")
    fine = Mesh(mesh.devices.reshape(ZH, ZL, C, Y, X), axes)
    placed = (
        P(axes, None),
        P(axes, None),
        P(axes, None),
        P(axes, None, None),
        P(axes, None),
    )
    return jax.shard_map(
        local, mesh=fine, in_specs=placed, out_specs=P(axes, None), check_vma=False
    )
```

```python
import functools
import math

import jax
import jax.numpy as jnp
from jax import lax
from jax.experimental import pallas as pl
from jax.experimental.pallas import tpu as pltpu
from jax.sharding import Mesh, PartitionSpec as P

KEY_HEADS = 4
GROUP = 5
WIDTH = 128
BLOCK = 128
LIST = 4
ZH, ZL, C, Y, X = 4, 4, 2, 4, 4
PEERS = ZL * C * Y * X
PEER_AXES = ("zl", "c", "y", "x")
KDEV = 64
NEAR = Y * X * KDEV
LANES = KEY_HEADS * 2 * WIDTH
PAIR = LANES // 2
TILES = PAIR // WIDTH
COPIES = Y * X
CHUNK = 8
SHARE = 2
PICKED = PEERS * LIST * SHARE
SCALE_LOG2 = math.log2(math.e) / math.sqrt(WIDTH)
MIB = 1024 * 1024
QROWS = GROUP * BLOCK


def stack_heads(q_ref):
    return jnp.concatenate([q_ref[:, h * WIDTH : (h + 1) * WIDTH] for h in range(GROUP)], axis=0)


def weigh(s, top):
    tiles = [
        jnp.exp2((s[:, k * WIDTH : (k + 1) * WIDTH] - top) * SCALE_LOG2)
        for k in range(s.shape[1] // WIDTH)
    ]
    return jnp.concatenate(tiles, axis=1).astype(jnp.bfloat16)


def row_top(s):
    top = s[:, :WIDTH]
    for k in range(1, s.shape[1] // WIDTH):
        top = jnp.maximum(top, s[:, k * WIDTH : (k + 1) * WIDTH])
    return jnp.broadcast_to(jnp.max(top, axis=1, keepdims=True), top.shape)


def weighted(w, v):
    ones = jnp.ones((v.shape[0], WIDTH), jnp.bfloat16)
    return jnp.dot(w, jnp.concatenate([v, ones], axis=1), preferred_element_type=jnp.float32)


def scores(q, k):
    return lax.dot_general(q, k, (((1,), (1,)), ((), ())), preferred_element_type=jnp.float32)


def diagonal():
    shape = (BLOCK, WIDTH)
    return lax.broadcasted_iota(jnp.int32, shape, 0) == lax.broadcasted_iota(jnp.int32, shape, 1)


def near_kernel(q_ref, k_ref, v_ref, mean_ref, log_ref):
    s = scores(stack_heads(q_ref), k_ref[...])
    top = row_top(s)
    both = weighted(weigh(s, top), v_ref[...])
    total = both[:, WIDTH:]
    mean_ref[0] = both[:, :WIDTH] / total
    log_ref[0] = jnp.zeros((8, WIDTH), jnp.float32)
    log = top + jnp.log2(total) * (1.0 / SCALE_LOG2)
    for h in range(GROUP):
        own = jnp.where(diagonal(), log[h * BLOCK : (h + 1) * BLOCK], 0.0)
        log_ref[0, h : h + 1] = jnp.sum(own, axis=0, keepdims=True)


def near_attention(queries, near):
    return pl.pallas_call(
        near_kernel,
        grid=(KEY_HEADS,),
        in_specs=[
            pl.BlockSpec((BLOCK, GROUP * WIDTH), lambda e: (0, e)),
            pl.BlockSpec((NEAR, WIDTH), lambda e: (0, 2 * e)),
            pl.BlockSpec((NEAR, WIDTH), lambda e: (0, 2 * e + 1)),
        ],
        out_specs=[
            pl.BlockSpec((1, QROWS, WIDTH), lambda e: (e, 0, 0)),
            pl.BlockSpec((1, 8, WIDTH), lambda e: (e, 0, 0)),
        ],
        out_shape=[
            pltpu.VMEM((KEY_HEADS, QROWS, WIDTH), jnp.float32),
            pltpu.VMEM((KEY_HEADS, 8, WIDTH), jnp.float32),
        ],
        compiler_params=pltpu.CompilerParams(vmem_limit_bytes=16 * MIB),
        cost_estimate=pl.CostEstimate(
            flops=200 * KEY_HEADS * QROWS * NEAR * WIDTH,
            bytes_accessed=8 * MIB,
            transcendentals=KEY_HEADS * QROWS * NEAR,
        ),
        name="near",
    )(
        pltpu.with_memory_space_constraint(queries, pltpu.HBM),
        pltpu.with_memory_space_constraint(near, pltpu.HBM),
        pltpu.with_memory_space_constraint(near, pltpu.HBM),
    )


def far_kernel(live_ref, q_ref, far_ref, mean_ref, log_ref, out_ref):
    column = lax.broadcasted_iota(jnp.int32, (1, LIST * BLOCK), 1)
    entry = (column % (LIST * SHARE)) // SHARE
    for e in range(KEY_HEADS):
        rows = slice(e // 2 * LIST * BLOCK, (e // 2 + 1) * LIST * BLOCK)
        k = far_ref[rows, 2 * (e % 2) * WIDTH : (2 * (e % 2) + 1) * WIDTH]
        v = far_ref[rows, (2 * (e % 2) + 1) * WIDTH : (2 * (e % 2) + 2) * WIDTH]
        q = stack_heads(q_ref.at[:, e * GROUP * WIDTH : (e + 1) * GROUP * WIDTH])
        s = jnp.where(entry < live_ref[e], scores(q, k), -1e30)
        near_log = jnp.concatenate(
            [
                jnp.broadcast_to(
                    jnp.sum(
                        jnp.where(diagonal(), log_ref[e, h : h + 1], 0.0), axis=1, keepdims=True
                    ),
                    (BLOCK, WIDTH),
                )
                for h in range(GROUP)
            ],
            axis=0,
        )
        top = jnp.maximum(near_log, row_top(s))
        back = jnp.exp2((near_log - top) * SCALE_LOG2)
        both = weighted(weigh(s, top), v)
        acc = back * mean_ref[e] + both[:, :WIDTH]
        total = back + both[:, WIDTH:]
        res = (acc / total).astype(jnp.bfloat16)
        for h in range(GROUP):
            head = slice((e * GROUP + h) * WIDTH, (e * GROUP + h + 1) * WIDTH)
            out_ref[:, head] = res[h * BLOCK : (h + 1) * BLOCK]


def far_attention(live, queries, far, mean, log):
    vmem = pl.BlockSpec(memory_space=pltpu.VMEM)
    return pl.pallas_call(
        far_kernel,
        in_specs=[pl.BlockSpec(memory_space=pltpu.SMEM), vmem, vmem, vmem, vmem],
        out_specs=vmem,
        out_shape=jax.ShapeDtypeStruct((BLOCK, KEY_HEADS * GROUP * WIDTH), jnp.bfloat16),
        compiler_params=pltpu.CompilerParams(vmem_limit_bytes=16 * MIB),
        name="far",
    )(
        live,
        queries,
        far,
        pltpu.with_memory_space_constraint(mean, pltpu.VMEM),
        pltpu.with_memory_space_constraint(log, pltpu.VMEM),
    )


def prep_kernel(ids_ref, k_ref, v_ref, near_ref, sent_ref):
    tiles = []
    for e in range(KEY_HEADS):
        tiles.append(k_ref[:, e * WIDTH : (e + 1) * WIDTH])
        tiles.append(v_ref[:, e * WIDTH : (e + 1) * WIDTH])
    own = jnp.concatenate(tiles, axis=1)
    for i in range(COPIES):
        near_ref[i * KDEV : (i + 1) * KDEV] = own
    shape = (KDEV * CHUNK, KDEV * TILES)
    row = lax.broadcasted_iota(jnp.int32, shape, 0)
    column = lax.broadcasted_iota(jnp.int32, shape, 1)
    target = jnp.where(row % CHUNK < TILES, row % CHUNK * KDEV + row // CHUNK, -1)
    hot = jnp.where(column == target, 1.0, 0.0).astype(jnp.bfloat16)
    shape = (KDEV * CHUNK, WIDTH)
    lane = lax.broadcasted_iota(jnp.int32, shape, 1)
    is_id = lax.broadcasted_iota(jnp.int32, shape, 0) % CHUNK >= TILES
    ids = jnp.zeros(shape, jnp.float32)
    for i in range(KEY_HEADS * LIST):
        ids = jnp.where(lane == i, ids_ref[i].astype(jnp.float32), ids)
    for j in range(2):
        moved = jnp.dot(
            hot,
            jnp.concatenate(tiles[j * TILES : (j + 1) * TILES], axis=0),
            preferred_element_type=jnp.float32,
        )
        rows = slice(j * KDEV * CHUNK, (j + 1) * KDEV * CHUNK)
        sent_ref[rows] = jnp.where(is_id, ids, moved).astype(jnp.bfloat16)


def prep(ids, keys, values):
    whole = lambda shape: pl.BlockSpec(shape, lambda i: (0, 0))
    return pl.pallas_call(
        prep_kernel,
        grid=(1,),
        in_specs=[
            pl.BlockSpec(memory_space=pltpu.SMEM),
            whole((KDEV, LANES // 2)),
            whole((KDEV, LANES // 2)),
        ],
        out_specs=[whole((COPIES * KDEV, LANES)), whole((PEERS * CHUNK, WIDTH))],
        out_shape=[
            jax.ShapeDtypeStruct((COPIES * KDEV, LANES), jnp.bfloat16),
            jax.ShapeDtypeStruct((PEERS * CHUNK, WIDTH), jnp.bfloat16),
        ],
        compiler_params=pltpu.CompilerParams(vmem_limit_bytes=16 * MIB),
        name="prep",
    )(
        ids,
        pltpu.with_memory_space_constraint(keys, pltpu.HBM),
        pltpu.with_memory_space_constraint(values, pltpu.HBM),
    )


def pick_kernel(index_ref, table_ref, out_ref):
    lane = lax.broadcasted_iota(jnp.int32, (PICKED, PEERS * ZH), 1)
    for e in range(2):
        hot = jnp.where(lane == index_ref[:, e : e + 1], 1.0, 0.0).astype(jnp.bfloat16)
        lanes = slice(2 * WIDTH * e, 2 * WIDTH * (e + 1))
        out_ref[:, lanes] = jnp.dot(
            hot, table_ref[:, lanes], preferred_element_type=jnp.float32
        ).astype(jnp.bfloat16)


def pick(index, table):
    return pl.pallas_call(
        pick_kernel,
        out_shape=jax.ShapeDtypeStruct((PICKED, PAIR), jnp.bfloat16),
        compiler_params=pltpu.CompilerParams(vmem_limit_bytes=16 * MIB),
        name="pick",
    )(index, table)


def local(queries, keys, values, far_blocks, far_live_length):
    near, sent = prep(far_blocks.reshape(KEY_HEADS * LIST), keys, values)
    near = lax.all_to_all(near, ("y", "x"), 0, 0, tiled=True)
    got = lax.all_to_all(sent.reshape(PEERS, CHUNK, WIDTH), PEER_AXES, 0, 0, tiled=True)
    table = lax.all_gather(got[:, :TILES].reshape(PEERS, PAIR), "zh", axis=0, tiled=True)

    asked = got[:, TILES, : KEY_HEADS * LIST].astype(jnp.int32).reshape(PEERS, 2, 2, LIST)
    asked = jnp.where(lax.axis_index("zl") < ZL // 2, asked[:, 0], asked[:, 1])
    half = jnp.arange(SHARE, dtype=jnp.int32).reshape(1, 1, SHARE, 1)
    index = asked.transpose(0, 2, 1)[:, :, None] * SHARE + half
    picked = pick(index.reshape(PICKED, 2), table)

    picked, queries = lax.optimization_barrier((picked, queries))
    arrived = lax.all_to_all(
        picked.reshape(PEERS, LIST * SHARE, PAIR), PEER_AXES, 0, 0, tiled=True
    )
    mean, log = near_attention(queries, near)
    live = far_live_length.reshape(KEY_HEADS)
    return far_attention(live, queries, arrived.reshape(PICKED, PAIR), mean, log)


def solution(mesh):
    axes = ("zh", "zl", "c", "y", "x")
    fine = Mesh(mesh.devices.reshape(ZH, ZL, C, Y, X), axes)
    placed = (
        P(axes, None),
        P(axes, None),
        P(axes, None),
        P(axes, None, None),
        P(axes, None),
    )
    return jax.shard_map(
        local, mesh=fine, in_specs=placed, out_specs=P(axes, None), check_vma=False
    )
```

```python
import functools
import math

import jax
import jax.numpy as jnp
from jax import lax
from jax.experimental import pallas as pl
from jax.experimental.pallas import tpu as pltpu
from jax.sharding import Mesh, PartitionSpec as P

KEY_HEADS = 4
GROUP = 5
WIDTH = 128
BLOCK = 128
LIST = 4
ZH, ZL, C, Y, X = 8, 2, 2, 4, 4
PEERS = ZL * C * Y * X
PEER_AXES = ("zl", "c", "y", "x")
KDEV = 64
NEAR = Y * X * KDEV
LANES = KEY_HEADS * 2 * WIDTH
PAIR = LANES // 2
TILES = PAIR // WIDTH
ROWS = 2
DATA = ROWS * TILES
UNIT = ROWS * PAIR
COPIES = Y * X
CHUNK = 16
SHARE = 2
SETS = 32
PICKED = PEERS * LIST * SHARE
SCALE_LOG2 = math.log2(math.e) / math.sqrt(WIDTH)
MIB = 1024 * 1024
QROWS = GROUP * BLOCK


def stack_heads(q_ref):
    return jnp.concatenate([q_ref[:, h * WIDTH : (h + 1) * WIDTH] for h in range(GROUP)], axis=0)


def weigh(s, top):
    tiles = [
        jnp.exp2((s[:, k * WIDTH : (k + 1) * WIDTH] - top) * SCALE_LOG2)
        for k in range(s.shape[1] // WIDTH)
    ]
    return jnp.concatenate(tiles, axis=1).astype(jnp.bfloat16)


def row_top(s):
    top = s[:, :WIDTH]
    for k in range(1, s.shape[1] // WIDTH):
        top = jnp.maximum(top, s[:, k * WIDTH : (k + 1) * WIDTH])
    return jnp.broadcast_to(jnp.max(top, axis=1, keepdims=True), top.shape)


def weighted(w, v):
    ones = jnp.ones((v.shape[0], WIDTH), jnp.bfloat16)
    return jnp.dot(w, jnp.concatenate([v, ones], axis=1), preferred_element_type=jnp.float32)


def scores(q, k):
    return lax.dot_general(q, k, (((1,), (1,)), ((), ())), preferred_element_type=jnp.float32)


def diagonal():
    shape = (BLOCK, WIDTH)
    return lax.broadcasted_iota(jnp.int32, shape, 0) == lax.broadcasted_iota(jnp.int32, shape, 1)


def near_kernel(q_ref, k_ref, v_ref, mean_ref, log_ref):
    s = scores(stack_heads(q_ref), k_ref[...])
    top = row_top(s)
    both = weighted(weigh(s, top), v_ref[...])
    total = both[:, WIDTH:]
    mean_ref[0] = both[:, :WIDTH] / total
    log_ref[0] = jnp.zeros((8, WIDTH), jnp.float32)
    log = top + jnp.log2(total) * (1.0 / SCALE_LOG2)
    for h in range(GROUP):
        own = jnp.where(diagonal(), log[h * BLOCK : (h + 1) * BLOCK], 0.0)
        log_ref[0, h : h + 1] = jnp.sum(own, axis=0, keepdims=True)


def near_attention(queries, near):
    return pl.pallas_call(
        near_kernel,
        grid=(KEY_HEADS,),
        in_specs=[
            pl.BlockSpec((BLOCK, GROUP * WIDTH), lambda e: (0, e)),
            pl.BlockSpec((NEAR, WIDTH), lambda e: (0, 2 * e)),
            pl.BlockSpec((NEAR, WIDTH), lambda e: (0, 2 * e + 1)),
        ],
        out_specs=[
            pl.BlockSpec((1, QROWS, WIDTH), lambda e: (e, 0, 0)),
            pl.BlockSpec((1, 8, WIDTH), lambda e: (e, 0, 0)),
        ],
        out_shape=[
            pltpu.VMEM((KEY_HEADS, QROWS, WIDTH), jnp.float32),
            pltpu.VMEM((KEY_HEADS, 8, WIDTH), jnp.float32),
        ],
        compiler_params=pltpu.CompilerParams(vmem_limit_bytes=16 * MIB),
        cost_estimate=pl.CostEstimate(
            flops=200 * KEY_HEADS * QROWS * NEAR * WIDTH,
            bytes_accessed=8 * MIB,
            transcendentals=KEY_HEADS * QROWS * NEAR,
        ),
        name="near",
    )(
        pltpu.with_memory_space_constraint(queries, pltpu.HBM),
        pltpu.with_memory_space_constraint(near, pltpu.HBM),
        pltpu.with_memory_space_constraint(near, pltpu.HBM),
    )


def far_kernel(live_ref, q_ref, far_ref, mean_ref, log_ref, out_hbm, out_ref, sems):
    copies = []
    column = lax.broadcasted_iota(jnp.int32, (1, LIST * BLOCK), 1)
    entry = (column % (LIST * SHARE)) // SHARE
    for e in range(KEY_HEADS):
        rows = slice(e // 2 * PICKED // 2, (e // 2 + 1) * PICKED // 2)
        tile = 2 * (e % 2)
        k, v = (
            jnp.concatenate(
                [
                    far_ref[rows, (r * TILES + t) * WIDTH : (r * TILES + t + 1) * WIDTH]
                    for r in range(ROWS)
                ],
                axis=0,
            )
            for t in (tile, tile + 1)
        )
        q = stack_heads(q_ref.at[:, e * GROUP * WIDTH : (e + 1) * GROUP * WIDTH])
        s = jnp.where(entry < live_ref[e], scores(q, k), -1e30)
        near_log = jnp.concatenate(
            [
                jnp.broadcast_to(
                    jnp.sum(
                        jnp.where(diagonal(), log_ref[e, h : h + 1], 0.0), axis=1, keepdims=True
                    ),
                    (BLOCK, WIDTH),
                )
                for h in range(GROUP)
            ],
            axis=0,
        )
        top = jnp.maximum(near_log, row_top(s))
        back = jnp.exp2((near_log - top) * SCALE_LOG2)
        both = weighted(weigh(s, top), v)
        acc = back * mean_ref[e] + both[:, :WIDTH]
        total = back + both[:, WIDTH:]
        res = (acc / total).astype(jnp.bfloat16)
        for h in range(GROUP):
            out_ref[e, :, h * WIDTH : (h + 1) * WIDTH] = res[h * BLOCK : (h + 1) * BLOCK]
        heads = slice(e * GROUP * WIDTH, (e + 1) * GROUP * WIDTH)
        copies.append(pltpu.make_async_copy(out_ref.at[e], out_hbm.at[:, heads], sems.at[e]))
        copies[-1].start()
    for copy in copies:
        copy.wait()


def far_attention(live, queries, far, mean, log):
    vmem = pl.BlockSpec(memory_space=pltpu.VMEM)
    return pl.pallas_call(
        far_kernel,
        in_specs=[pl.BlockSpec(memory_space=pltpu.SMEM), vmem, vmem, vmem, vmem],
        out_specs=pl.BlockSpec(memory_space=pl.ANY),
        out_shape=jax.ShapeDtypeStruct((BLOCK, KEY_HEADS * GROUP * WIDTH), jnp.bfloat16),
        scratch_shapes=[
            pltpu.VMEM((KEY_HEADS, BLOCK, GROUP * WIDTH), jnp.bfloat16),
            pltpu.SemaphoreType.DMA((KEY_HEADS,)),
        ],
        compiler_params=pltpu.CompilerParams(vmem_limit_bytes=16 * MIB),
        name="far",
    )(
        live,
        queries,
        far,
        pltpu.with_memory_space_constraint(mean, pltpu.VMEM),
        pltpu.with_memory_space_constraint(log, pltpu.VMEM),
    )


def prep_kernel(ids_ref, k_ref, v_ref, sent_ref):
    tiles = []
    for e in range(KEY_HEADS):
        tiles.append(k_ref[:, e * WIDTH : (e + 1) * WIDTH])
        tiles.append(v_ref[:, e * WIDTH : (e + 1) * WIDTH])
    shape = (KDEV // ROWS * CHUNK, KDEV * TILES)
    row = lax.broadcasted_iota(jnp.int32, shape, 0)
    column = lax.broadcasted_iota(jnp.int32, shape, 1)
    place = row % CHUNK
    target = place % TILES * KDEV + row // CHUNK * ROWS + place // TILES
    target = jnp.where(place < DATA, target, -1)
    hot = jnp.where(column == target, 1.0, 0.0).astype(jnp.bfloat16)
    shape = (KDEV // ROWS * CHUNK, WIDTH)
    lane = lax.broadcasted_iota(jnp.int32, shape, 1)
    is_id = lax.broadcasted_iota(jnp.int32, shape, 0) % CHUNK >= DATA
    ids = jnp.zeros(shape, jnp.float32)
    for i in range(KEY_HEADS * LIST):
        ids = jnp.where(lane == i, ids_ref[0, i // LIST, i % LIST].astype(jnp.float32), ids)
    for j in range(2):
        moved = jnp.dot(
            hot,
            jnp.concatenate(tiles[j * TILES : (j + 1) * TILES], axis=0),
            preferred_element_type=jnp.float32,
        )
        rows = slice(j * KDEV // ROWS * CHUNK, (j + 1) * KDEV // ROWS * CHUNK)
        sent_ref[rows] = jnp.where(is_id, ids, moved).astype(jnp.bfloat16)


def copies_kernel(k_ref, v_ref, near_hbm, own_ref, sems):
    tiles = []
    for e in range(KEY_HEADS):
        tiles.append(k_ref[:, e * WIDTH : (e + 1) * WIDTH])
        tiles.append(v_ref[:, e * WIDTH : (e + 1) * WIDTH])
    own_ref[...] = jnp.concatenate(tiles, axis=1)
    moves = [
        pltpu.make_async_copy(own_ref, near_hbm.at[i * KDEV : (i + 1) * KDEV], sems.at[i])
        for i in range(COPIES)
    ]
    for move in moves:
        move.start()
    for move in moves:
        move.wait()


def copies(keys, values):
    whole = pl.BlockSpec((KDEV, LANES // 2), lambda i: (0, 0))
    return pl.pallas_call(
        copies_kernel,
        grid=(1,),
        in_specs=[whole, whole],
        out_specs=pl.BlockSpec(memory_space=pl.ANY),
        out_shape=jax.ShapeDtypeStruct((COPIES * KDEV, LANES), jnp.bfloat16),
        scratch_shapes=[
            pltpu.VMEM((KDEV, LANES), jnp.bfloat16),
            pltpu.SemaphoreType.DMA((COPIES,)),
        ],
        name="copies",
    )(
        pltpu.with_memory_space_constraint(keys, pltpu.HBM),
        pltpu.with_memory_space_constraint(values, pltpu.HBM),
    )


def prep(ids, keys, values):
    whole = lambda shape: pl.BlockSpec(shape, lambda i: (0, 0))
    return pl.pallas_call(
        prep_kernel,
        grid=(1,),
        in_specs=[
            pl.BlockSpec(memory_space=pltpu.SMEM),
            whole((KDEV, LANES // 2)),
            whole((KDEV, LANES // 2)),
        ],
        out_specs=whole((PEERS * CHUNK, WIDTH)),
        out_shape=jax.ShapeDtypeStruct((PEERS * CHUNK, WIDTH), jnp.bfloat16),
        compiler_params=pltpu.CompilerParams(vmem_limit_bytes=16 * MIB),
        name="prep",
    )(
        ids,
        pltpu.with_memory_space_constraint(keys, pltpu.HBM),
        pltpu.with_memory_space_constraint(values, pltpu.HBM),
    )


def pick_kernel(index_ref, *refs):
    units, out_ref = refs[:-1], refs[-1]
    lane = lax.broadcasted_iota(jnp.int32, (PICKED, PEERS * ZH), 1)
    table = jnp.concatenate([unit[...] for unit in units], axis=0)
    for e in range(2):
        hot = jnp.where(lane == index_ref[:, e : e + 1], 1.0, 0.0).astype(jnp.bfloat16)
        for r in range(ROWS):
            lanes = slice(r * PAIR + 2 * WIDTH * e, r * PAIR + 2 * WIDTH * (e + 1))
            out_ref[:, lanes] = jnp.dot(
                hot, table[:, lanes], preferred_element_type=jnp.float32
            ).astype(jnp.bfloat16)


def pick(index, units):
    return pl.pallas_call(
        pick_kernel,
        out_shape=pltpu.VMEM((PICKED, UNIT), jnp.bfloat16),
        compiler_params=pltpu.CompilerParams(vmem_limit_bytes=16 * MIB),
        name="pick",
    )(index, *units)


def gather_sets(unit):
    up = [(k, (k + 1) % ZH) for k in range(ZH)]
    down = [(k, (k - 1) % ZH) for k in range(ZH)]
    ups, downs = [unit], [unit]
    for _ in range(ZH // 2 - 1):
        ups.append(lax.ppermute(ups[-1], "zh", up))
        downs.append(lax.ppermute(downs[-1], "zh", down))
    middle = PEERS // 2
    first = lax.ppermute(ups[-1][:middle], "zh", up)
    second = lax.ppermute(downs[-1][middle:], "zh", down)
    return downs + [first, second] + ups[:0:-1]


def local(queries, keys, values, far_blocks, far_live_length):
    sent = prep(far_blocks, keys, values)
    near = copies(keys, values)
    near = lax.all_to_all(near, ("y", "x"), 0, 0, tiled=True)
    got = lax.all_to_all(sent.reshape(PEERS, CHUNK, WIDTH), PEER_AXES, 0, 0, tiled=True)
    units = gather_sets(got[:, :DATA].reshape(PEERS, UNIT))

    asked = got[:, DATA, : KEY_HEADS * LIST].astype(jnp.int32).reshape(PEERS, 2, 2, LIST)
    asked = jnp.where(lax.axis_index("zl") < ZL // 2, asked[:, 0], asked[:, 1])
    place = (asked // SETS - lax.axis_index("zh")) % ZH
    half = jnp.arange(SHARE, dtype=jnp.int32).reshape(1, 1, SHARE, 1)
    row = place * PEERS + asked % SETS * SHARE
    index = row.transpose(0, 2, 1)[:, :, None] + half
    picked = pick(index.reshape(PICKED, 2), units)

    picked, queries = lax.optimization_barrier((picked, queries))
    arrived = lax.all_to_all(
        picked.reshape(PEERS, LIST * SHARE, UNIT), PEER_AXES, 0, 0, tiled=True
    )
    mean, log = near_attention(queries, near)
    live = far_live_length.reshape(KEY_HEADS)
    return far_attention(live, queries, arrived.reshape(PICKED, UNIT), mean, log)


def solution(mesh):
    axes = ("zh", "zl", "c", "y", "x")
    fine = Mesh(mesh.devices.reshape(ZH, ZL, C, Y, X), axes)
    placed = (
        P(axes, None),
        P(axes, None),
        P(axes, None),
        P(axes, None, None),
        P(axes, None),
    )
    return jax.shard_map(
        local, mesh=fine, in_specs=placed, out_specs=P(axes, None), check_vma=False
    )
```

```python
import functools
import math

import jax
import jax.numpy as jnp
from jax import lax
from jax.experimental import pallas as pl
from jax.experimental.pallas import tpu as pltpu
from jax.sharding import Mesh, PartitionSpec as P

KEY_HEADS = 4
GROUP = 5
WIDTH = 128
BLOCK = 128
LIST = 4
ZH, ZL, C, Y, X = 8, 2, 2, 4, 4
PEERS = ZL * C * Y * X
PEER_AXES = ("zl", "c", "y", "x")
KDEV = 64
NEAR = Y * X * KDEV
LANES = KEY_HEADS * 2 * WIDTH
PAIR = LANES // 2
TILES = PAIR // WIDTH
ROWS = 2
DATA = ROWS * TILES
UNIT = ROWS * PAIR
COPIES = Y * X
CHUNK = 16
SHARE = 2
SETS = 32
PICKED = PEERS * LIST * SHARE
SCALE_LOG2 = math.log2(math.e) / math.sqrt(WIDTH)
MIB = 1024 * 1024
QROWS = GROUP * BLOCK


def stack_heads(q_ref):
    return jnp.concatenate([q_ref[:, h * WIDTH : (h + 1) * WIDTH] for h in range(GROUP)], axis=0)


def weigh(s, top):
    tiles = [
        jnp.exp2((s[:, k * WIDTH : (k + 1) * WIDTH] - top) * SCALE_LOG2)
        for k in range(s.shape[1] // WIDTH)
    ]
    return jnp.concatenate(tiles, axis=1).astype(jnp.bfloat16)


def row_top(s):
    top = s[:, :WIDTH]
    for k in range(1, s.shape[1] // WIDTH):
        top = jnp.maximum(top, s[:, k * WIDTH : (k + 1) * WIDTH])
    return jnp.broadcast_to(jnp.max(top, axis=1, keepdims=True), top.shape)


def weighted(w, v):
    ones = jnp.ones((v.shape[0], WIDTH), jnp.bfloat16)
    return jnp.dot(w, jnp.concatenate([v, ones], axis=1), preferred_element_type=jnp.float32)


def scores(q, k):
    return lax.dot_general(q, k, (((1,), (1,)), ((), ())), preferred_element_type=jnp.float32)


def diagonal():
    shape = (BLOCK, WIDTH)
    return lax.broadcasted_iota(jnp.int32, shape, 0) == lax.broadcasted_iota(jnp.int32, shape, 1)


def near_kernel(q_ref, k_ref, v_ref, mean_ref, log_ref):
    s = scores(stack_heads(q_ref), k_ref[...])
    top = row_top(s)
    both = weighted(weigh(s, top), v_ref[...])
    total = both[:, WIDTH:]
    mean_ref[0] = both[:, :WIDTH] / total
    log_ref[0] = jnp.zeros((8, WIDTH), jnp.float32)
    log = top + jnp.log2(total) * (1.0 / SCALE_LOG2)
    for h in range(GROUP):
        own = jnp.where(diagonal(), log[h * BLOCK : (h + 1) * BLOCK], 0.0)
        log_ref[0, h : h + 1] = jnp.sum(own, axis=0, keepdims=True)


def near_attention(queries, near):
    return pl.pallas_call(
        near_kernel,
        grid=(KEY_HEADS,),
        in_specs=[
            pl.BlockSpec((BLOCK, GROUP * WIDTH), lambda e: (0, e)),
            pl.BlockSpec((NEAR, WIDTH), lambda e: (0, 2 * e)),
            pl.BlockSpec((NEAR, WIDTH), lambda e: (0, 2 * e + 1)),
        ],
        out_specs=[
            pl.BlockSpec((1, QROWS, WIDTH), lambda e: (e, 0, 0)),
            pl.BlockSpec((1, 8, WIDTH), lambda e: (e, 0, 0)),
        ],
        out_shape=[
            pltpu.VMEM((KEY_HEADS, QROWS, WIDTH), jnp.float32),
            pltpu.VMEM((KEY_HEADS, 8, WIDTH), jnp.float32),
        ],
        compiler_params=pltpu.CompilerParams(vmem_limit_bytes=16 * MIB),
        cost_estimate=pl.CostEstimate(
            flops=200 * KEY_HEADS * QROWS * NEAR * WIDTH,
            bytes_accessed=8 * MIB,
            transcendentals=KEY_HEADS * QROWS * NEAR,
        ),
        name="near",
    )(
        pltpu.with_memory_space_constraint(queries, pltpu.HBM),
        pltpu.with_memory_space_constraint(near, pltpu.HBM),
        pltpu.with_memory_space_constraint(near, pltpu.HBM),
    )


def far_kernel(live_ref, q_ref, far_ref, mean_ref, log_ref, out_hbm, out_ref, sems):
    copies = []
    column = lax.broadcasted_iota(jnp.int32, (1, LIST * BLOCK), 1)
    entry = (column % (LIST * SHARE)) // SHARE
    for e in range(KEY_HEADS):
        rows = slice(e // 2 * PICKED // 2, (e // 2 + 1) * PICKED // 2)
        tile = 2 * (e % 2)
        k, v = (
            jnp.concatenate(
                [
                    far_ref[rows, (r * TILES + t) * WIDTH : (r * TILES + t + 1) * WIDTH]
                    for r in range(ROWS)
                ],
                axis=0,
            )
            for t in (tile, tile + 1)
        )
        q = stack_heads(q_ref.at[:, e * GROUP * WIDTH : (e + 1) * GROUP * WIDTH])
        s = jnp.where(entry < live_ref[e], scores(q, k), -1e30)
        near_log = jnp.concatenate(
            [
                jnp.broadcast_to(
                    jnp.sum(
                        jnp.where(diagonal(), log_ref[e, h : h + 1], 0.0), axis=1, keepdims=True
                    ),
                    (BLOCK, WIDTH),
                )
                for h in range(GROUP)
            ],
            axis=0,
        )
        top = jnp.maximum(near_log, row_top(s))
        back = jnp.exp2((near_log - top) * SCALE_LOG2)
        both = weighted(weigh(s, top), v)
        acc = back * mean_ref[e] + both[:, :WIDTH]
        total = back + both[:, WIDTH:]
        res = (acc / total).astype(jnp.bfloat16)
        for h in range(GROUP):
            out_ref[e, :, h * WIDTH : (h + 1) * WIDTH] = res[h * BLOCK : (h + 1) * BLOCK]
        heads = slice(e * GROUP * WIDTH, (e + 1) * GROUP * WIDTH)
        copies.append(pltpu.make_async_copy(out_ref.at[e], out_hbm.at[:, heads], sems.at[e]))
        copies[-1].start()
    for copy in copies:
        copy.wait()


def far_attention(live, queries, far, mean, log):
    vmem = pl.BlockSpec(memory_space=pltpu.VMEM)
    return pl.pallas_call(
        far_kernel,
        in_specs=[pl.BlockSpec(memory_space=pltpu.SMEM), vmem, vmem, vmem, vmem],
        out_specs=pl.BlockSpec(memory_space=pl.ANY),
        out_shape=jax.ShapeDtypeStruct((BLOCK, KEY_HEADS * GROUP * WIDTH), jnp.bfloat16),
        scratch_shapes=[
            pltpu.VMEM((KEY_HEADS, BLOCK, GROUP * WIDTH), jnp.bfloat16),
            pltpu.SemaphoreType.DMA((KEY_HEADS,)),
        ],
        compiler_params=pltpu.CompilerParams(vmem_limit_bytes=16 * MIB),
        name="far",
    )(
        live,
        queries,
        far,
        pltpu.with_memory_space_constraint(mean, pltpu.VMEM),
        pltpu.with_memory_space_constraint(log, pltpu.VMEM),
    )


def prep_kernel(ids_ref, k_ref, v_ref, sent_ref):
    tiles = []
    for e in range(KEY_HEADS):
        tiles.append(k_ref[:, e * WIDTH : (e + 1) * WIDTH])
        tiles.append(v_ref[:, e * WIDTH : (e + 1) * WIDTH])
    shape = (KDEV // ROWS * CHUNK, KDEV * TILES)
    row = lax.broadcasted_iota(jnp.int32, shape, 0)
    column = lax.broadcasted_iota(jnp.int32, shape, 1)
    place = row % CHUNK
    target = place % TILES * KDEV + row // CHUNK * ROWS + place // TILES
    target = jnp.where(place < DATA, target, -1)
    hot = jnp.where(column == target, 1.0, 0.0).astype(jnp.bfloat16)
    shape = (KDEV // ROWS * CHUNK, WIDTH)
    lane = lax.broadcasted_iota(jnp.int32, shape, 1)
    is_id = lax.broadcasted_iota(jnp.int32, shape, 0) % CHUNK >= DATA
    ids = jnp.zeros(shape, jnp.float32)
    for i in range(KEY_HEADS * LIST):
        ids = jnp.where(lane == i, ids_ref[0, i // LIST, i % LIST].astype(jnp.float32), ids)
    for j in range(2):
        moved = jnp.dot(
            hot,
            jnp.concatenate(tiles[j * TILES : (j + 1) * TILES], axis=0),
            preferred_element_type=jnp.float32,
        )
        rows = slice(j * KDEV // ROWS * CHUNK, (j + 1) * KDEV // ROWS * CHUNK)
        sent_ref[rows] = jnp.where(is_id, ids, moved).astype(jnp.bfloat16)


def copies_kernel(k_ref, v_ref, near_hbm, own_ref, sems):
    tiles = []
    for e in range(KEY_HEADS):
        tiles.append(k_ref[:, e * WIDTH : (e + 1) * WIDTH])
        tiles.append(v_ref[:, e * WIDTH : (e + 1) * WIDTH])
    own_ref[...] = jnp.concatenate(tiles, axis=1)
    moves = [
        pltpu.make_async_copy(own_ref, near_hbm.at[i * KDEV : (i + 1) * KDEV], sems.at[i])
        for i in range(COPIES)
    ]
    for move in moves:
        move.start()
    for move in moves:
        move.wait()


def copies(keys, values):
    whole = pl.BlockSpec((KDEV, LANES // 2), lambda i: (0, 0))
    return pl.pallas_call(
        copies_kernel,
        grid=(1,),
        in_specs=[whole, whole],
        out_specs=pl.BlockSpec(memory_space=pl.ANY),
        out_shape=jax.ShapeDtypeStruct((COPIES * KDEV, LANES), jnp.bfloat16),
        scratch_shapes=[
            pltpu.VMEM((KDEV, LANES), jnp.bfloat16),
            pltpu.SemaphoreType.DMA((COPIES,)),
        ],
        name="copies",
    )(
        pltpu.with_memory_space_constraint(keys, pltpu.HBM),
        pltpu.with_memory_space_constraint(values, pltpu.HBM),
    )


def prep(ids, keys, values):
    whole = lambda shape: pl.BlockSpec(shape, lambda i: (0, 0))
    return pl.pallas_call(
        prep_kernel,
        grid=(1,),
        in_specs=[
            pl.BlockSpec((1, KEY_HEADS, LIST), lambda i: (0, 0, 0), memory_space=pltpu.SMEM),
            whole((KDEV, LANES // 2)),
            whole((KDEV, LANES // 2)),
        ],
        out_specs=whole((PEERS * CHUNK, WIDTH)),
        out_shape=pltpu.VMEM((PEERS * CHUNK, WIDTH), jnp.bfloat16),
        compiler_params=pltpu.CompilerParams(vmem_limit_bytes=16 * MIB),
        name="prep",
    )(
        pltpu.with_memory_space_constraint(ids, pltpu.HBM),
        pltpu.with_memory_space_constraint(keys, pltpu.HBM),
        pltpu.with_memory_space_constraint(values, pltpu.HBM),
    )


def pick_kernel(index_ref, *refs):
    units, out_ref = refs[:-1], refs[-1]
    lane = lax.broadcasted_iota(jnp.int32, (PICKED, PEERS * ZH), 1)
    table = jnp.concatenate([unit[...] for unit in units], axis=0)
    for e in range(2):
        hot = jnp.where(lane == index_ref[:, e : e + 1], 1.0, 0.0).astype(jnp.bfloat16)
        for r in range(ROWS):
            lanes = slice(r * PAIR + 2 * WIDTH * e, r * PAIR + 2 * WIDTH * (e + 1))
            out_ref[:, lanes] = jnp.dot(
                hot, table[:, lanes], preferred_element_type=jnp.float32
            ).astype(jnp.bfloat16)


def pick(index, units):
    return pl.pallas_call(
        pick_kernel,
        out_shape=pltpu.VMEM((PICKED, UNIT), jnp.bfloat16),
        compiler_params=pltpu.CompilerParams(vmem_limit_bytes=16 * MIB),
        name="pick",
    )(index, *units)


def gather_sets(unit):
    up = [(k, (k + 1) % ZH) for k in range(ZH)]
    down = [(k, (k - 1) % ZH) for k in range(ZH)]
    ups, downs = [unit], [unit]
    for step in range(ZH // 2):
        ups.append(lax.ppermute(ups[-1], "zh", up))
        if step < ZH // 2 - 1:
            downs.append(lax.ppermute(downs[-1], "zh", down))
    return downs + ups[:0:-1]


def local(queries, keys, values, far_blocks, far_live_length):
    sent = prep(far_blocks, keys, values)
    near = copies(keys, values)
    near = lax.all_to_all(near, ("y", "x"), 0, 0, tiled=True)
    got = lax.all_to_all(sent.reshape(PEERS, CHUNK, WIDTH), PEER_AXES, 0, 0, tiled=True)
    units = gather_sets(got[:, :DATA].reshape(PEERS, UNIT))

    asked = got[:, DATA, : KEY_HEADS * LIST].astype(jnp.int32).reshape(PEERS, 2, 2, LIST)
    asked = jnp.where(lax.axis_index("zl") < ZL // 2, asked[:, 0], asked[:, 1])
    place = (asked // SETS - lax.axis_index("zh")) % ZH
    half = jnp.arange(SHARE, dtype=jnp.int32).reshape(1, 1, SHARE, 1)
    row = place * PEERS + asked % SETS * SHARE
    index = row.transpose(0, 2, 1)[:, :, None] + half
    picked = pick(index.reshape(PICKED, 2), units)

    picked, queries = lax.optimization_barrier((picked, queries))
    arrived = lax.all_to_all(
        picked.reshape(PEERS, LIST * SHARE, UNIT), PEER_AXES, 0, 0, tiled=True
    )
    mean, log = near_attention(queries, near)
    live = far_live_length.reshape(KEY_HEADS)
    return far_attention(live, queries, arrived.reshape(PICKED, UNIT), mean, log)


def solution(mesh):
    axes = ("zh", "zl", "c", "y", "x")
    fine = Mesh(mesh.devices.reshape(ZH, ZL, C, Y, X), axes)
    placed = (
        P(axes, None),
        P(axes, None),
        P(axes, None),
        P(axes, None, None),
        P(axes, None),
    )
    return jax.shard_map(
        local, mesh=fine, in_specs=placed, out_specs=P(axes, None), check_vma=False
    )
```

```python
import functools
import math

import jax
import jax.numpy as jnp
from jax import lax
from jax.experimental import pallas as pl
from jax.experimental.pallas import tpu as pltpu
from jax.sharding import Mesh, PartitionSpec as P

KEY_HEADS = 4
GROUP = 5
WIDTH = 128
BLOCK = 128
LIST = 4
ZH, ZL, C, Y, X = 8, 2, 2, 4, 4
PEERS = ZL * C * Y * X
PEER_AXES = ("zl", "c", "y", "x")
KDEV = 64
NEAR = Y * X * KDEV
LANES = KEY_HEADS * 2 * WIDTH
PAIR = LANES // 2
TILES = PAIR // WIDTH
ROWS = 2
DATA = ROWS * TILES
UNIT = ROWS * PAIR
COPIES = Y * X
CHUNK = 16
SHARE = 2
LAST = ZH // 2
SETS = 32
PICKED = PEERS * LIST * SHARE
SCALE_LOG2 = math.log2(math.e) / math.sqrt(WIDTH)
MIB = 1024 * 1024
QROWS = GROUP * BLOCK


def stack_heads(q_ref):
    return jnp.concatenate([q_ref[:, h * WIDTH : (h + 1) * WIDTH] for h in range(GROUP)], axis=0)


def weigh(s, top):
    tiles = [
        jnp.exp2((s[:, k * WIDTH : (k + 1) * WIDTH] - top) * SCALE_LOG2)
        for k in range(s.shape[1] // WIDTH)
    ]
    return jnp.concatenate(tiles, axis=1).astype(jnp.bfloat16)


def row_top(s):
    top = s[:, :WIDTH]
    for k in range(1, s.shape[1] // WIDTH):
        top = jnp.maximum(top, s[:, k * WIDTH : (k + 1) * WIDTH])
    return jnp.broadcast_to(jnp.max(top, axis=1, keepdims=True), top.shape)


def weighted(w, v):
    ones = jnp.ones((v.shape[0], WIDTH), jnp.bfloat16)
    return jnp.dot(w, jnp.concatenate([v, ones], axis=1), preferred_element_type=jnp.float32)


def scores(q, k):
    return lax.dot_general(q, k, (((1,), (1,)), ((), ())), preferred_element_type=jnp.float32)


def diagonal():
    shape = (BLOCK, WIDTH)
    return lax.broadcasted_iota(jnp.int32, shape, 0) == lax.broadcasted_iota(jnp.int32, shape, 1)


def near_kernel(q_ref, k_ref, v_ref, mean_ref, log_ref):
    s = scores(stack_heads(q_ref), k_ref[...])
    top = row_top(s)
    both = weighted(weigh(s, top), v_ref[...])
    total = both[:, WIDTH:]
    mean_ref[0] = both[:, :WIDTH] / total
    log_ref[0] = jnp.zeros((8, WIDTH), jnp.float32)
    log = top + jnp.log2(total) * (1.0 / SCALE_LOG2)
    for h in range(GROUP):
        own = jnp.where(diagonal(), log[h * BLOCK : (h + 1) * BLOCK], 0.0)
        log_ref[0, h : h + 1] = jnp.sum(own, axis=0, keepdims=True)


def near_attention(queries, near):
    return pl.pallas_call(
        near_kernel,
        grid=(KEY_HEADS,),
        in_specs=[
            pl.BlockSpec((BLOCK, GROUP * WIDTH), lambda e: (0, e)),
            pl.BlockSpec((NEAR, WIDTH), lambda e: (0, 2 * e)),
            pl.BlockSpec((NEAR, WIDTH), lambda e: (0, 2 * e + 1)),
        ],
        out_specs=[
            pl.BlockSpec((1, QROWS, WIDTH), lambda e: (e, 0, 0)),
            pl.BlockSpec((1, 8, WIDTH), lambda e: (e, 0, 0)),
        ],
        out_shape=[
            pltpu.VMEM((KEY_HEADS, QROWS, WIDTH), jnp.float32),
            pltpu.VMEM((KEY_HEADS, 8, WIDTH), jnp.float32),
        ],
        compiler_params=pltpu.CompilerParams(vmem_limit_bytes=16 * MIB),
        cost_estimate=pl.CostEstimate(
            flops=200 * KEY_HEADS * QROWS * NEAR * WIDTH,
            bytes_accessed=8 * MIB,
            transcendentals=KEY_HEADS * QROWS * NEAR,
        ),
        name="near",
    )(
        pltpu.with_memory_space_constraint(queries, pltpu.HBM),
        pltpu.with_memory_space_constraint(near, pltpu.HBM),
        pltpu.with_memory_space_constraint(near, pltpu.HBM),
    )


def far_kernel(live_ref, q_ref, far_ref, mean_ref, log_ref, out_hbm, out_ref, sems):
    copies = []
    column = lax.broadcasted_iota(jnp.int32, (1, LIST * BLOCK), 1)
    entry = (column % (LIST * SHARE)) // SHARE
    for e in range(KEY_HEADS):
        rows = slice(e // 2 * PICKED // 2, (e // 2 + 1) * PICKED // 2)
        tile = 2 * (e % 2)
        k, v = (
            jnp.concatenate(
                [
                    far_ref[rows, (r * TILES + t) * WIDTH : (r * TILES + t + 1) * WIDTH]
                    for r in range(ROWS)
                ],
                axis=0,
            )
            for t in (tile, tile + 1)
        )
        q = stack_heads(q_ref.at[:, e * GROUP * WIDTH : (e + 1) * GROUP * WIDTH])
        s = jnp.where(entry < live_ref[e], scores(q, k), -1e30)
        near_log = jnp.concatenate(
            [
                jnp.broadcast_to(
                    jnp.sum(
                        jnp.where(diagonal(), log_ref[e, h : h + 1], 0.0), axis=1, keepdims=True
                    ),
                    (BLOCK, WIDTH),
                )
                for h in range(GROUP)
            ],
            axis=0,
        )
        top = jnp.maximum(near_log, row_top(s))
        back = jnp.exp2((near_log - top) * SCALE_LOG2)
        both = weighted(weigh(s, top), v)
        acc = back * mean_ref[e] + both[:, :WIDTH]
        total = back + both[:, WIDTH:]
        res = (acc / total).astype(jnp.bfloat16)
        for h in range(GROUP):
            out_ref[e, :, h * WIDTH : (h + 1) * WIDTH] = res[h * BLOCK : (h + 1) * BLOCK]
        heads = slice(e * GROUP * WIDTH, (e + 1) * GROUP * WIDTH)
        copies.append(pltpu.make_async_copy(out_ref.at[e], out_hbm.at[:, heads], sems.at[e]))
        copies[-1].start()
    for copy in copies:
        copy.wait()


def far_attention(live, queries, far, mean, log):
    vmem = pl.BlockSpec(memory_space=pltpu.VMEM)
    return pl.pallas_call(
        far_kernel,
        in_specs=[pl.BlockSpec(memory_space=pltpu.SMEM), vmem, vmem, vmem, vmem],
        out_specs=pl.BlockSpec(memory_space=pl.ANY),
        out_shape=jax.ShapeDtypeStruct((BLOCK, KEY_HEADS * GROUP * WIDTH), jnp.bfloat16),
        scratch_shapes=[
            pltpu.VMEM((KEY_HEADS, BLOCK, GROUP * WIDTH), jnp.bfloat16),
            pltpu.SemaphoreType.DMA((KEY_HEADS,)),
        ],
        compiler_params=pltpu.CompilerParams(vmem_limit_bytes=16 * MIB),
        name="far",
    )(
        live,
        queries,
        far,
        pltpu.with_memory_space_constraint(mean, pltpu.VMEM),
        pltpu.with_memory_space_constraint(log, pltpu.VMEM),
    )


def prep_kernel(ids_ref, k_ref, v_ref, sent_ref):
    tiles = []
    for e in range(KEY_HEADS):
        tiles.append(k_ref[:, e * WIDTH : (e + 1) * WIDTH])
        tiles.append(v_ref[:, e * WIDTH : (e + 1) * WIDTH])
    shape = (KDEV // ROWS * CHUNK, KDEV * TILES)
    row = lax.broadcasted_iota(jnp.int32, shape, 0)
    column = lax.broadcasted_iota(jnp.int32, shape, 1)
    place = row % CHUNK
    target = place % TILES * KDEV + row // CHUNK * ROWS + place // TILES
    target = jnp.where(place < DATA, target, -1)
    hot = jnp.where(column == target, 1.0, 0.0).astype(jnp.bfloat16)
    shape = (KDEV // ROWS * CHUNK, WIDTH)
    lane = lax.broadcasted_iota(jnp.int32, shape, 1)
    is_id = lax.broadcasted_iota(jnp.int32, shape, 0) % CHUNK >= DATA
    ids = jnp.zeros(shape, jnp.float32)
    for i in range(KEY_HEADS * LIST):
        ids = jnp.where(lane == i, ids_ref[0, i // LIST, i % LIST].astype(jnp.float32), ids)
    for j in range(2):
        moved = jnp.dot(
            hot,
            jnp.concatenate(tiles[j * TILES : (j + 1) * TILES], axis=0),
            preferred_element_type=jnp.float32,
        )
        rows = slice(j * KDEV // ROWS * CHUNK, (j + 1) * KDEV // ROWS * CHUNK)
        sent_ref[rows] = jnp.where(is_id, ids, moved).astype(jnp.bfloat16)


def copies_kernel(k_ref, v_ref, near_hbm, own_ref, sems):
    tiles = []
    for e in range(KEY_HEADS):
        tiles.append(k_ref[:, e * WIDTH : (e + 1) * WIDTH])
        tiles.append(v_ref[:, e * WIDTH : (e + 1) * WIDTH])
    own_ref[...] = jnp.concatenate(tiles, axis=1)
    moves = [
        pltpu.make_async_copy(own_ref, near_hbm.at[i * KDEV : (i + 1) * KDEV], sems.at[i])
        for i in range(COPIES)
    ]
    for move in moves:
        move.start()
    for move in moves:
        move.wait()


def copies(keys, values):
    whole = pl.BlockSpec((KDEV, LANES // 2), lambda i: (0, 0))
    return pl.pallas_call(
        copies_kernel,
        grid=(1,),
        in_specs=[whole, whole],
        out_specs=pl.BlockSpec(memory_space=pl.ANY),
        out_shape=jax.ShapeDtypeStruct((COPIES * KDEV, LANES), jnp.bfloat16),
        scratch_shapes=[
            pltpu.VMEM((KDEV, LANES), jnp.bfloat16),
            pltpu.SemaphoreType.DMA((COPIES,)),
        ],
        name="copies",
    )(
        pltpu.with_memory_space_constraint(keys, pltpu.HBM),
        pltpu.with_memory_space_constraint(values, pltpu.HBM),
    )


def prep(ids, keys, values):
    whole = lambda shape: pl.BlockSpec(shape, lambda i: (0, 0))
    return pl.pallas_call(
        prep_kernel,
        grid=(1,),
        in_specs=[
            pl.BlockSpec((1, KEY_HEADS, LIST), lambda i: (0, 0, 0), memory_space=pltpu.SMEM),
            whole((KDEV, LANES // 2)),
            whole((KDEV, LANES // 2)),
        ],
        out_specs=whole((PEERS * CHUNK, WIDTH)),
        out_shape=pltpu.VMEM((PEERS * CHUNK, WIDTH), jnp.bfloat16),
        compiler_params=pltpu.CompilerParams(vmem_limit_bytes=16 * MIB),
        name="prep",
    )(
        pltpu.with_memory_space_constraint(ids, pltpu.HBM),
        pltpu.with_memory_space_constraint(keys, pltpu.HBM),
        pltpu.with_memory_space_constraint(values, pltpu.HBM),
    )


def chosen(index_ref, e, lane):
    return jnp.where(lane == index_ref[:, e : e + 1], 1.0, 0.0).astype(jnp.bfloat16)


def unit_lanes(e, r):
    return slice(r * PAIR + 2 * WIDTH * e, r * PAIR + 2 * WIDTH * (e + 1))


def pick_kernel(index_ref, *refs):
    units, out_ref = refs[:-1], refs[-1]
    lane = lax.broadcasted_iota(jnp.int32, (PICKED, PEERS * (ZH - 1)), 1)
    lane = jnp.where(lane >= PEERS * LAST, lane + PEERS, lane)
    table = jnp.concatenate([unit[...] for unit in units], axis=0)
    for e in range(2):
        hot = chosen(index_ref, e, lane)
        for r in range(ROWS):
            lanes = unit_lanes(e, r)
            out_ref[:, lanes] = jnp.dot(
                hot, table[:, lanes], preferred_element_type=jnp.float32
            ).astype(jnp.bfloat16)


def pick_last_kernel(index_ref, part_ref, unit_ref, out_ref):
    lane = lax.broadcasted_iota(jnp.int32, (PICKED, PEERS), 1) + PEERS * LAST
    for e in range(2):
        hot = chosen(index_ref, e, lane)
        for r in range(ROWS):
            lanes = unit_lanes(e, r)
            own = jnp.dot(hot, unit_ref[:, lanes], preferred_element_type=jnp.float32)
            out_ref[:, lanes] = part_ref[:, lanes] + own.astype(jnp.bfloat16)


def pick(index, units):
    arguments = dict(
        out_shape=pltpu.VMEM((PICKED, UNIT), jnp.bfloat16),
        compiler_params=pltpu.CompilerParams(vmem_limit_bytes=16 * MIB),
    )
    part = pl.pallas_call(pick_kernel, name="pick", **arguments)(
        index, *units[:LAST], *units[LAST + 1 :]
    )
    return pl.pallas_call(pick_last_kernel, name="pick_last", **arguments)(
        index, part, units[LAST]
    )


def gather_sets(unit):
    up = [(k, (k + 1) % ZH) for k in range(ZH)]
    down = [(k, (k - 1) % ZH) for k in range(ZH)]
    ups, downs = [unit], [unit]
    for step in range(ZH // 2):
        ups.append(lax.ppermute(ups[-1], "zh", up))
        if step < ZH // 2 - 1:
            downs.append(lax.ppermute(downs[-1], "zh", down))
    return downs + ups[:0:-1]


def local(queries, keys, values, far_blocks, far_live_length):
    sent = prep(far_blocks, keys, values)
    near = copies(keys, values)
    near = lax.all_to_all(near, ("y", "x"), 0, 0, tiled=True)
    got = lax.all_to_all(sent.reshape(PEERS, CHUNK, WIDTH), PEER_AXES, 0, 0, tiled=True)
    units = gather_sets(got[:, :DATA].reshape(PEERS, UNIT))

    asked = got[:, DATA, : KEY_HEADS * LIST].astype(jnp.int32).reshape(PEERS, 2, 2, LIST)
    asked = jnp.where(lax.axis_index("zl") < ZL // 2, asked[:, 0], asked[:, 1])
    place = (asked // SETS - lax.axis_index("zh")) % ZH
    half = jnp.arange(SHARE, dtype=jnp.int32).reshape(1, 1, SHARE, 1)
    row = place * PEERS + asked % SETS * SHARE
    index = row.transpose(0, 2, 1)[:, :, None] + half
    picked = pick(index.reshape(PICKED, 2), units)

    picked, queries = lax.optimization_barrier((picked, queries))
    arrived = lax.all_to_all(
        picked.reshape(PEERS, LIST * SHARE, UNIT), PEER_AXES, 0, 0, tiled=True
    )
    mean, log = near_attention(queries, near)
    live = far_live_length.reshape(KEY_HEADS)
    return far_attention(live, queries, arrived.reshape(PICKED, UNIT), mean, log)


def solution(mesh):
    axes = ("zh", "zl", "c", "y", "x")
    fine = Mesh(mesh.devices.reshape(ZH, ZL, C, Y, X), axes)
    placed = (
        P(axes, None),
        P(axes, None),
        P(axes, None),
        P(axes, None, None),
        P(axes, None),
    )
    return jax.shard_map(
        local, mesh=fine, in_specs=placed, out_specs=P(axes, None), check_vma=False
    )
```
